32 devices in a mesh: module: 4 (over y, core), sample: 8 (over z, x).
Axes of the slice: x: 2, y: 2, z: 4, core: 2. Of those that a mesh axis runs over, the one named last changes fastest.
Arguments:
- queries: bfloat16 [16, 256, 4096], P('module', None, 'sample'), may hold values from -6 to 6
- inverse_hessian: bfloat16 [16, 4096, 4096], P('module', 'sample'), may hold values from -1 to 2.1, as said below
- train_grads: bfloat16 [16, 2560, 4096], P('module', 'sample'), may hold values from -0.09375 to 0.09375
Outputs:
- scores: float32 [2560, 256], P('sample')
The draws below stay inside these ranges and needn't reach their ends.
Inputs may be any that keep to these rules, and one draw needn't show every extreme that they name: `inverse_hessian`: each module's matrix is symmetric.
All inputs are finite; a program needn't handle non-finite values.
Results may differ from the reference program's by a relative error of at most 0.0029.
Values may be sent and summed in bfloat16 or wider, within the bound.
A program may use at most 64 MiB of HBM per device.

```python
import math
import jax
import jax.numpy as jnp
from jax import lax

K = 4096
Q = 256
M = 16
S = 2560


def draw_inverse_hessian(key, part):
    noise_key = jax.random.fold_in(key, 11)
    diag_key = jax.random.fold_in(key, 12)
    noise = jax.random.normal(noise_key, (M, K, K), jnp.float32)
    lower, upper = (math.log(0.5), math.log(2.0))
    symmetric = (noise + jnp.swapaxes(noise, 1, 2)) * (0.35 * K ** (-0.5))
    diag_vals = jnp.exp(jax.random.uniform(diag_key, (M, K), jnp.float32, lower, upper))
    ident = jnp.eye(K, dtype=jnp.float32)
    return (symmetric + diag_vals[:, :, None] * ident[None, :, :]).astype(jnp.bfloat16)


def levels(key, dims, pieces, low, largest):
    gain, own = 1.0, jax.random.fold_in(key, 6)
    for position, shards_of in pieces:
        draws = jnp.exp(jax.random.uniform(jax.random.fold_in(own, position), (shards_of,), jnp.float32, low / len(pieces), largest / len(pieces)))
        gain = gain * jnp.repeat(draws, dims[position] // shards_of).reshape([-1 if axis == position else 1 for axis in range(len(dims))])
    return gain


def bell_draw(key, extent, scale, limit, shards=(), kind=jnp.bfloat16):
    drawn = jax.random.normal(key, extent, jnp.float32) * scale
    if len(shards) > 0:
        drawn = levels(key, extent, shards, -0.22, 0.18) * drawn
    return jnp.clip(drawn, min=-limit, max=limit).astype(kind)


def setup_inputs(seed: int = 0) -> dict:
    keys = jax.random.split(jax.random.key(seed), 4)
    queries = bell_draw(keys[0], (M, Q, K), 1.0, 6.0, ((0, 4), (2, 8)))
    inverse_hessian = draw_inverse_hessian(jax.random.fold_in(keys[3], 71), 0)
    train_grads = bell_draw(keys[2], (M, S, K), K ** -0.5, 0.09375, ((0, 4), (1, 8)))
    return dict(queries=queries, inverse_hessian=inverse_hessian, train_grads=train_grads)


def reference(queries, inverse_hessian, train_grads):
    def add_module(index, total):
        query = queries[index]
        matrix = inverse_hessian[index]
        grads = train_grads[index]
        precond = jnp.dot(query, matrix, preferred_element_type=jnp.float32).astype(jnp.bfloat16)
        return total + lax.dot_general(grads, precond, (((1,), (1,)), ((), ())), preferred_element_type=jnp.float32)

    start = jnp.zeros((train_grads.shape[1], queries.shape[1]), jnp.float32)
    return lax.fori_loop(0, queries.shape[0], add_module, start)
```

```python
import functools

import jax
import jax.numpy as jnp
from jax import lax
from jax.experimental import pallas as pl
from jax.experimental.pallas import tpu as pltpu
from jax.sharding import PartitionSpec as P

PAIR = 2
ROWS = 16
LANES = 128
NT = (((1,), (1,)), ((), ()))


def by_symmetry(query, slab, grads):
    share = lax.dot_general(
        slab,
        lax.all_gather(query, "sample", axis=1, tiled=True),
        NT,
        preferred_element_type=jnp.float32,
    ).astype(jnp.bfloat16)
    return jnp.dot(
        grads,
        lax.all_gather(share, "sample", axis=0, tiled=True),
        preferred_element_type=jnp.float32,
    )


def by_gather(queries, inverse_hessian, train_grads):
    total = jnp.zeros((train_grads.shape[1], queries.shape[1]), jnp.float32)
    for module_idx in range(queries.shape[0]):
        total = total + by_symmetry(
            queries[module_idx], inverse_hessian[module_idx], train_grads[module_idx]
        )
    return lax.psum(total, "module")


def pieces_of(rows):
    cross = rows * 3 // 16 // ROWS * ROWS
    half = (rows - cross + 1) // 2
    half = (half + ROWS - 1) // ROWS * ROWS
    return ((0, half, False), (half, rows - cross - half, False), (rows - cross, cross, True))


def ladder(
    n, q_hbm, h_hbm, g_hbm, out_ref, blocks, h, g, acc, recv, zsend, xsend, q_sem, h_sem, g_sem
):
    modules, rows, wide = q_hbm.shape
    items = 2 * modules
    levels = n // PAIR
    pieces = pieces_of(rows)
    me = lax.axis_index("sample")
    z, x = me // PAIR, me % PAIR
    other = 1 - x

    q_loads = [
        pltpu.make_async_copy(q_hbm.at[m], blocks.at[m, me], q_sem.at[m]) for m in range(modules)
    ]
    for load in q_loads:
        load.start()
    for m in range(modules):
        pltpu.make_async_copy(h_hbm.at[m], h.at[m], h_sem.at[m]).start()
    for m in range(modules):
        pltpu.make_async_copy(g_hbm.at[m], g.at[m], g_sem.at[m]).start()

    barrier = pltpu.get_barrier_semaphore()
    greeted = (
        lax.rem(z + 1, levels) * PAIR + x,
        lax.rem(z + levels - 1, levels) * PAIR + x,
        z * PAIR + other,
    )
    for device in greeted:
        pl.semaphore_signal(
            barrier, inc=1, device_id={"sample": device}, device_id_type=pl.DeviceIdType.MESH
        )
    pl.semaphore_wait(barrier, len(greeted))

    out_ref[...] = jnp.zeros_like(out_ref)
    for load in q_loads:
        load.wait()

    def copy(i, p, level, column, sem, device):
        first, count, _ = pieces[p]
        slot = level * PAIR + column
        ref = blocks.at[i, slot, pl.ds(first, count)]
        return pltpu.make_async_remote_copy(
            src_ref=ref,
            dst_ref=ref,
            send_sem=sem,
            recv_sem=recv.at[i, p, slot],
            device_id={"sample": device},
            device_id_type=pl.DeviceIdType.MESH,
        )

    def up(i, p, level, column, act):
        @pl.when(z < levels - 1)
        def _():
            act(copy(i, p, level, column, zsend.at[i, p, column, level], me + PAIR))

    def down(i, p, level, column, act):
        @pl.when(z > 0)
        def _():
            act(copy(i, p, level, column, zsend.at[i, p, column, level + 1], me - PAIR))

    def across(i, p, level, act):
        act(copy(i, p, level, x, xsend.at[i, p, level], z * PAIR + other))

    def arrived(i, p, level, column):
        copy(i, p, level, column, xsend.at[i, p, level], me).wait_recv()

    def own(i, act):
        for p in range(len(pieces)):
            up(i, p, z, x, act)
            down(i, p, z, x, act)
            across(i, p, z, act)

    def relay(i, act, wait):
        for p, (_, _, crosses) in enumerate(pieces):
            if crosses:
                if wait:
                    arrived(i, p, z, other)
                up(i, p, z, other, act)
                down(i, p, z, other, act)
        for d in range(1, levels):
            for p, (_, _, crosses) in enumerate(pieces):

                @pl.when(z >= d)
                def _():
                    for column in (x, other) if crosses else (x,):
                        if wait:
                            arrived(i, p, z - d, column)
                        up(i, p, z - d, column, act)
                    if not crosses:
                        across(i, p, z - d, act)

                @pl.when(z + d < levels)
                def _():
                    for column in (x, other) if crosses else (x,):
                        if wait:
                            arrived(i, p, z + d, column)
                        down(i, p, z + d, column, act)
                    if not crosses:
                        across(i, p, z + d, act)

    def crossed(i):
        for p, (_, _, crosses) in enumerate(pieces):
            if not crosses:
                for level in range(levels):
                    arrived(i, p, level, other)

    def columns(s):
        return pl.ds(pl.multiple_of(s * wide, LANES), wide)

    def precondition(m):
        pltpu.make_async_copy(h_hbm.at[m], h.at[m], h_sem.at[m]).wait()
        acc[...] = jnp.zeros_like(acc)

        @pl.loop(0, n)
        def _(s):
            acc[...] += lax.dot_general(
                blocks[m, s], h[m, :, columns(s)], NT, preferred_element_type=jnp.float32
            )

        blocks[modules + m, me] = acc[...].astype(blocks.dtype)

    def score(m):
        pltpu.make_async_copy(g_hbm.at[m], g.at[m], g_sem.at[m]).wait()

        @pl.loop(0, n)
        def _(s):
            out_ref[...] += lax.dot_general(
                g[m, :, columns(s)], blocks[modules + m, s], NT, preferred_element_type=jnp.float32
            )

    own(0, lambda c: c.start())

    @pl.loop(0, items + 1)
    def _(t):
        @pl.when(t + 1 < items)
        def _():
            own(t + 1, lambda c: c.start())

        @pl.when(t < items)
        def _():
            relay(t, lambda c: c.start(), True)

        @pl.when(t > 0)
        def _():
            crossed(t - 1)

        @pl.when((t > 0) & (t <= modules))
        def _():
            precondition(t - 1)

        @pl.when(t > modules)
        def _():
            score(t - 1 - modules)

    @pl.loop(0, items)
    def _(t):
        own(t, lambda c: c.wait_send())
        relay(t, lambda c: c.wait_send(), False)


def by_ladder(n, queries, inverse_hessian, train_grads):
    modules, rows, wide = queries.shape
    samples, depth = train_grads.shape[1:]
    levels = n // PAIR
    items = 2 * modules
    count = len(pieces_of(rows))
    kind = queries.dtype
    total = pl.pallas_call(
        functools.partial(ladder, n),
        out_shape=jax.ShapeDtypeStruct((samples, rows), jnp.float32),
        in_specs=[pl.BlockSpec(memory_space=pl.ANY)] * 3,
        out_specs=pl.BlockSpec(memory_space=pltpu.VMEM),
        scratch_shapes=[
            pltpu.VMEM((items, n, rows, wide), kind),
            pltpu.VMEM((modules, wide, depth), kind),
            pltpu.VMEM((modules, samples, depth), kind),
            pltpu.VMEM((rows, wide), jnp.float32),
            pltpu.SemaphoreType.DMA((items, count, n)),
            pltpu.SemaphoreType.DMA((items, count, PAIR, levels + 1)),
            pltpu.SemaphoreType.DMA((items, count, levels)),
            pltpu.SemaphoreType.DMA((modules,)),
            pltpu.SemaphoreType.DMA((modules,)),
            pltpu.SemaphoreType.DMA((modules,)),
        ],
        compiler_params=pltpu.CompilerParams(
            collective_id=0, has_side_effects=True, vmem_limit_bytes=56 * 2**20
        ),
    )(queries, inverse_hessian, train_grads)
    return lax.psum(total, "module")


def solution(mesh):
    n = mesh.shape["sample"]

    def on_device(queries, inverse_hessian, train_grads):
        _, rows, wide = queries.shape
        if wide % LANES or rows % ROWS or n % PAIR or n <= 2 * PAIR:
            return by_gather(queries, inverse_hessian, train_grads)
        return by_ladder(n, queries, inverse_hessian, train_grads)

    placed = (P("module", None, "sample"), P("module", "sample", None), P("module", "sample", None))
    return jax.shard_map(
        on_device, mesh=mesh, in_specs=placed, out_specs=P("sample", None), check_vma=False
    )
```

```python
import functools

import jax
import jax.numpy as jnp
from jax import lax
from jax.experimental import pallas as pl
from jax.experimental.pallas import tpu as pltpu
from jax.sharding import PartitionSpec as P

PAIR = 2
ROWS = 16
LANES = 128
AHEAD = 2
NT = (((1,), (1,)), ((), ()))


def by_symmetry(query, slab, grads):
    share = lax.dot_general(
        slab,
        lax.all_gather(query, "sample", axis=1, tiled=True),
        NT,
        preferred_element_type=jnp.float32,
    ).astype(jnp.bfloat16)
    return jnp.dot(
        grads,
        lax.all_gather(share, "sample", axis=0, tiled=True),
        preferred_element_type=jnp.float32,
    )


def by_gather(queries, inverse_hessian, train_grads):
    total = jnp.zeros((train_grads.shape[1], queries.shape[1]), jnp.float32)
    for module_idx in range(queries.shape[0]):
        total = total + by_symmetry(
            queries[module_idx], inverse_hessian[module_idx], train_grads[module_idx]
        )
    return lax.psum(total, "module")


def pieces_of(rows):
    cross = rows * 3 // 16 // ROWS * ROWS
    half = (rows - cross + 1) // 2
    half = (half + ROWS - 1) // ROWS * ROWS
    return ((0, half, False), (half, rows - cross - half, False), (rows - cross, cross, True))


def ladder(
    n, q_hbm, h_hbm, g_hbm, out_ref, blocks, h, g, acc, halves, recv, zsend, xsend, q_sem, h_sem, g_sem, sum_send, sum_recv
):
    modules, rows, wide = q_hbm.shape
    items = 2 * modules
    levels = n // PAIR
    pieces = pieces_of(rows)
    me = lax.axis_index("sample")
    z, x = me // PAIR, me % PAIR
    other = 1 - x

    q_loads = [
        pltpu.make_async_copy(q_hbm.at[m], blocks.at[m, me], q_sem.at[m]) for m in range(modules)
    ]
    for load in q_loads:
        load.start()
    for m in range(modules):
        pltpu.make_async_copy(h_hbm.at[m], h.at[m], h_sem.at[m]).start()
    for m in range(modules):
        pltpu.make_async_copy(g_hbm.at[m], g.at[m], g_sem.at[m]).start()

    barrier = pltpu.get_barrier_semaphore()
    greeted = (
        lax.rem(z + 1, levels) * PAIR + x,
        lax.rem(z + levels - 1, levels) * PAIR + x,
        z * PAIR + other,
    )
    group = lax.axis_index("module")
    chip, core = group // PAIR, group % PAIR
    twin = chip * PAIR + 1 - core
    beyond = (1 - chip) * PAIR + core
    for device in greeted:
        pl.semaphore_signal(
            barrier, inc=1, device_id={"sample": device}, device_id_type=pl.DeviceIdType.MESH
        )
    for device in (twin, beyond):
        pl.semaphore_signal(
            barrier, inc=1, device_id={"module": device}, device_id_type=pl.DeviceIdType.MESH
        )
    pl.semaphore_wait(barrier, len(greeted) + 2)

    out_ref[...] = jnp.zeros_like(out_ref)
    for load in q_loads:
        load.wait()

    def copy(i, p, level, column, sem, device):
        first, count, _ = pieces[p]
        slot = level * PAIR + column
        ref = blocks.at[i, slot, pl.ds(first, count)]
        return pltpu.make_async_remote_copy(
            src_ref=ref,
            dst_ref=ref,
            send_sem=sem,
            recv_sem=recv.at[i, p, slot],
            device_id={"sample": device},
            device_id_type=pl.DeviceIdType.MESH,
        )

    def up(i, p, level, column, act):
        @pl.when(z < levels - 1)
        def _():
            act(copy(i, p, level, column, zsend.at[i, p, column, level], me + PAIR))

    def down(i, p, level, column, act):
        @pl.when(z > 0)
        def _():
            act(copy(i, p, level, column, zsend.at[i, p, column, level + 1], me - PAIR))

    def across(i, p, level, act):
        act(copy(i, p, level, x, xsend.at[i, p, level], z * PAIR + other))

    def arrived(i, p, level, column):
        copy(i, p, level, column, xsend.at[i, p, level], me).wait_recv()

    def own(i, act):
        for p in range(len(pieces)):
            up(i, p, z, x, act)
            down(i, p, z, x, act)
            across(i, p, z, act)

    def relay(i, act, wait):
        for p, (_, _, crosses) in enumerate(pieces):
            if crosses:
                if wait:
                    arrived(i, p, z, other)
                up(i, p, z, other, act)
                down(i, p, z, other, act)
        for d in range(1, levels):
            for p, (_, _, crosses) in enumerate(pieces):

                @pl.when(z >= d)
                def _():
                    for column in (x, other) if crosses else (x,):
                        if wait:
                            arrived(i, p, z - d, column)
                        up(i, p, z - d, column, act)
                    if not crosses:
                        across(i, p, z - d, act)

                @pl.when(z + d < levels)
                def _():
                    for column in (x, other) if crosses else (x,):
                        if wait:
                            arrived(i, p, z + d, column)
                        down(i, p, z + d, column, act)
                    if not crosses:
                        across(i, p, z + d, act)

    def crossed(i):
        for p, (_, _, crosses) in enumerate(pieces):
            if not crosses:
                for level in range(levels):
                    arrived(i, p, level, other)

    def columns(s):
        return pl.ds(pl.multiple_of(s * wide, LANES), wide)

    def precondition(m):
        pltpu.make_async_copy(h_hbm.at[m], h.at[m], h_sem.at[m]).wait()
        acc[...] = jnp.zeros_like(acc)

        @pl.loop(0, n)
        def _(s):
            acc[...] += lax.dot_general(
                blocks[m, s], h[m, :, columns(s)], NT, preferred_element_type=jnp.float32
            )

        blocks[modules + m, me] = acc[...].astype(blocks.dtype)

    def score(m):
        pltpu.make_async_copy(g_hbm.at[m], g.at[m], g_sem.at[m]).wait()

        @pl.loop(0, n)
        def _(s):
            out_ref[...] += lax.dot_general(
                g[m, :, columns(s)], blocks[modules + m, s], NT, preferred_element_type=jnp.float32
            )

    ahead = min(AHEAD, modules - 2)
    for i in range(ahead):
        own(i, lambda c: c.start())

    @pl.loop(0, items + 1)
    def _(t):
        @pl.when(t + ahead < items)
        def _():
            own(t + ahead, lambda c: c.start())

        @pl.when(t < items)
        def _():
            relay(t, lambda c: c.start(), True)

        @pl.when(t > 0)
        def _():
            crossed(t - 1)

        @pl.when((t > 0) & (t <= modules))
        def _():
            precondition(t - 1)

        @pl.when(t > modules)
        def _():
            score(t - 1 - modules)

    half = out_ref.shape[0] // PAIR
    kept = pl.ds(pl.multiple_of(core * half, 8), half)
    given = pl.ds(pl.multiple_of((1 - core) * half, 8), half)

    def exchange(step, rows, device):
        move = pltpu.make_async_remote_copy(
            src_ref=out_ref.at[rows],
            dst_ref=halves.at[step],
            send_sem=sum_send.at[step],
            recv_sem=sum_recv.at[step],
            device_id={"module": device},
            device_id_type=pl.DeviceIdType.MESH,
        )
        move.start()
        move.wait()

    exchange(0, given, twin)
    out_ref[kept] += halves[0]
    exchange(1, kept, beyond)
    out_ref[kept] += halves[1]
    exchange(2, kept, twin)
    out_ref[given] = halves[2]

    @pl.loop(0, items)
    def _(t):
        own(t, lambda c: c.wait_send())
        relay(t, lambda c: c.wait_send(), False)


def by_ladder(n, queries, inverse_hessian, train_grads):
    modules, rows, wide = queries.shape
    samples, depth = train_grads.shape[1:]
    levels = n // PAIR
    items = 2 * modules
    count = len(pieces_of(rows))
    kind = queries.dtype
    return pl.pallas_call(
        functools.partial(ladder, n),
        out_shape=jax.ShapeDtypeStruct((samples, rows), jnp.float32),
        in_specs=[pl.BlockSpec(memory_space=pl.ANY)] * 3,
        out_specs=pl.BlockSpec(memory_space=pltpu.VMEM),
        scratch_shapes=[
            pltpu.VMEM((items, n, rows, wide), kind),
            pltpu.VMEM((modules, wide, depth), kind),
            pltpu.VMEM((modules, samples, depth), kind),
            pltpu.VMEM((rows, wide), jnp.float32),
            pltpu.VMEM((3, samples // PAIR, rows), jnp.float32),
            pltpu.SemaphoreType.DMA((items, count, n)),
            pltpu.SemaphoreType.DMA((items, count, PAIR, levels + 1)),
            pltpu.SemaphoreType.DMA((items, count, levels)),
            pltpu.SemaphoreType.DMA((modules,)),
            pltpu.SemaphoreType.DMA((modules,)),
            pltpu.SemaphoreType.DMA((modules,)),
            pltpu.SemaphoreType.DMA((3,)),
            pltpu.SemaphoreType.DMA((3,)),
        ],
        compiler_params=pltpu.CompilerParams(
            collective_id=0, has_side_effects=True, vmem_limit_bytes=56 * 2**20
        ),
    )(queries, inverse_hessian, train_grads)


def solution(mesh):
    n, groups = mesh.shape["sample"], mesh.shape["module"]

    def on_device(queries, inverse_hessian, train_grads):
        modules, rows, wide = queries.shape
        aligned = wide % LANES == 0 and rows % ROWS == 0 and train_grads.shape[1] % ROWS == 0
        ladders = n % PAIR == 0 and n > 2 * PAIR and groups == PAIR * PAIR
        if not (aligned and ladders and modules > 2):
            return by_gather(queries, inverse_hessian, train_grads)
        return by_ladder(n, queries, inverse_hessian, train_grads)

    placed = (P("module", None, "sample"), P("module", "sample", None), P("module", "sample", None))
    return jax.shard_map(
        on_device, mesh=mesh, in_specs=placed, out_specs=P("sample", None), check_vma=False
    )
```
